128 devices in a mesh: wide: 16 (over z, x), narrow: 8 (over y, core).
Axes of the slice: x: 4, y: 4, z: 4, core: 2. Of those that a mesh axis runs over, the one named last changes fastest.
Arguments:
- coeffs: float32 [24, 64, 131072], P(None, None, ('wide', 'narrow')), may hold values from -6 to 6
- phases: float32 [6, 24, 131072], P(None, None, ('wide', 'narrow')), may hold values from -3.140625 to 3.140625
- mixers: float32 [6, 2, 2, 24, 24], replicated, may hold values from -1.25 to 1.25
Outputs:
- result: float32 [24, 64, 131072], P(None, None, ('wide', 'narrow'))
The draws below stay inside these ranges and needn't reach their ends.
All inputs are finite; a program needn't handle non-finite values.
Results may differ from the reference program's by a relative error of at most 0.0003.
Values sent between devices are 32-bit elements; how exact they have to be, the bound alone decides.
A program may use at most 128 MiB of HBM per device.

```python
import jax
import jax.numpy as jnp
from jax import lax

RANK = 24
COLS = 64
BLK_DEV = 1024
LEVELS = 6
NBLK = 131072
N_WIDE = 16
N_NARROW = 8


def level_of(key, dims, pieces, smallest, largest):
    factor_of, own = 1.0, jax.random.fold_in(key, 6)
    for dim, parts in pieces:
        draws = jnp.exp(jax.random.uniform(jax.random.fold_in(own, dim), (parts,), jnp.float32, smallest / len(pieces), largest / len(pieces)))
        factor_of = factor_of * jnp.repeat(draws, dims[dim] // parts).reshape([-1 if axis == dim else 1 for axis in range(len(dims))])
    return factor_of


def noise(own_key, shape, deviation, most, split=(), kind=jnp.bfloat16):
    result = deviation * jax.random.normal(own_key, shape, jnp.float32)
    if split:
        result = result * level_of(own_key, shape, split, -0.22, 0.18)
    return jnp.clip(result, -most, most).astype(kind)


def setup_inputs(seed: int = 0) -> dict:
    arg_keys = jax.random.split(jax.random.key(seed), 4)
    return {
        "coeffs": noise(arg_keys[0], (RANK, COLS, NBLK), 1.0, 6.0, ((2, 128),), jnp.float32),
        "phases": jnp.clip(jax.random.uniform(arg_keys[1], (LEVELS, RANK, NBLK), jnp.float32, -3.140625, 3.140625), -3.140625, 3.140625),
        "mixers": noise(arg_keys[2], (LEVELS, 2, 2, RANK, RANK), RANK ** -0.5, 1.25, (), jnp.float32),
    }


def combine_level(field, angle, mixing, position):
    rank_size, col_size, total = field.shape
    low = 2 ** position
    shaped = field.reshape(rank_size, col_size, total // (2 * low), 2, low)
    angled = angle.reshape(rank_size, total // (2 * low), 2, low)
    first = shaped[:, :, :, 0, :]
    second = shaped[:, :, :, 1, :]
    outputs = []
    for side in range(2):
        summed = jnp.einsum("ar,rcbk->acbk", mixing[side, 0], first, precision=lax.Precision.HIGHEST)
        summed = summed + jnp.einsum("ar,rcbk->acbk", mixing[side, 1], second, precision=lax.Precision.HIGHEST)
        outputs.append(jnp.cos(angled[:, :, side, :])[:, None, :, :] * summed)
    return jnp.stack(outputs, axis=3).reshape(rank_size, col_size, total)


def reference(coeffs, phases, mixers):
    log_blk = BLK_DEV.bit_length() - 1
    log_near = N_NARROW.bit_length() - 1
    log_wide = N_WIDE.bit_length() - 1
    far_base = log_blk + log_near + log_wide - 3
    positions = [log_blk, log_blk + log_near - 1, log_blk - 1, far_base, far_base + 1, far_base + 2]
    field = coeffs
    for level in range(LEVELS):
        field = combine_level(field, phases[level], mixers[level], positions[level])
    return field
```

```python
import functools

import jax
import jax.numpy as jnp
from jax import lax
from jax.experimental import pallas as pl
from jax.experimental.pallas import tpu as pltpu
from jax.sharding import PartitionSpec as P

MESH = pl.DeviceIdType.MESH
SUB = 8
SPLITS = 2
WIDTH = 256 // SPLITS


def split(x):
    high = x.astype(jnp.bfloat16)
    return high, (x - high.astype(jnp.float32)).astype(jnp.bfloat16)


def mixed(w, own, other):
    rows = own.shape[0]
    own_high, own_low = split(own)
    other_high, other_low = split(other)
    high = jnp.concatenate([own_high, other_high], axis=0)
    low = jnp.concatenate([own_low, other_low], axis=0)
    both = jnp.dot(w[...], high, preferred_element_type=jnp.float32)
    rest = jnp.dot(w[:rows], low, preferred_element_type=jnp.float32)
    return both[:rows] + (both[rows:] + rest)


def scaled(value, angle):
    rank, width = angle.shape
    return (value.reshape(rank, SUB, width) * angle[:, None, :]).reshape(rank * SUB, width)


def kernel(
    chunks, rank, coeffs, phases, mixers, out, a, b, c_core, c_y, c_x, c_z, weights, cosines, z_cos,
    load_sem, core_send, core_recv, y_send, y_recv, x_send, x_recv, z_send, z_recv,
    back_send, back_recv, keep_sem, cos_send, cos_recv,
):
    wide, narrow = lax.axis_index("wide"), lax.axis_index("narrow")
    here = wide // 4
    core_peer, y_peer, x_peer = (wide, narrow ^ 1), (wide, narrow ^ 4), (wide ^ 2, narrow)
    z_peers = [(wide ^ (4 * p), narrow) for p in (1, 2, 3)]

    barrier = pltpu.get_barrier_semaphore()
    peers = [core_peer, y_peer, x_peer, *z_peers]
    for peer in peers:
        pl.semaphore_signal(barrier, inc=1, device_id=peer, device_id_type=MESH)
    pl.semaphore_wait(barrier, len(peers))

    def window(ref, k, q):
        group, part = k // SPLITS, k % SPLITS
        columns = pl.ds(pl.multiple_of(group * SUB, SUB), SUB)
        start = (q // 2) * 512 + part * (2 * WIDTH) + (q % 2) * WIDTH
        return ref.at[:, columns, pl.ds(pl.multiple_of(start, WIDTH), WIDTH)]

    def remote(src, dst, send, recv, peer):
        return pltpu.make_async_remote_copy(src, dst, send, recv, device_id=peer, device_id_type=MESH)

    def load(k, q):
        return pltpu.make_async_copy(window(coeffs, k, q), a.at[k, q], load_sem.at[k, q])

    def core_copy(k, q):
        return remote(window(coeffs, k, q), c_core.at[k, q], core_send.at[k, q], core_recv.at[k, q], core_peer)

    def y_copy(k):
        return remote(b.at[k], c_y.at[k], y_send.at[k], y_recv.at[k], y_peer)

    def x_copy(k):
        return remote(a.at[k], c_x.at[k], x_send.at[k], x_recv.at[k], x_peer)

    def z_copy(k, p):
        there = here ^ p
        return remote(b.at[k, there], c_z.at[k, here], z_send.at[k, p - 1], z_recv.at[k, p - 1], z_peers[p - 1])

    def back_copy(k, p):
        there = here ^ p
        return remote(a.at[k, there], window(out, k, here), back_send.at[k, p - 1], back_recv.at[k, p - 1], z_peers[p - 1])

    def keep_copy(k):
        return pltpu.make_async_copy(a.at[k, here], window(out, k, here), keep_sem.at[k])

    def cos_copy(p):
        there = here ^ p
        return remote(
            cosines.at[:, there, pl.ds(4, 2)], z_cos.at[here], cos_send.at[p - 1], cos_recv.at[p - 1], z_peers[p - 1]
        )

    def send_core(k, carry):
        for q in range(4):
            core_copy(k, q).start()
            load(k, q).start()
        return carry

    lax.fori_loop(0, chunks, send_core, 0)

    rows = rank * SUB

    def take_cosines(level):
        value = jnp.cos(phases[level])
        for part in range(SPLITS):
            for q in range(4):
                start = (q // 2) * 512 + part * (2 * WIDTH) + (q % 2) * WIDTH
                cosines[part, q, level] = value[:, start : start + WIDTH]

    spread = (
        lax.broadcasted_iota(jnp.int32, (2 * rank, 2 * rows), 0)
        == lax.broadcasted_iota(jnp.int32, (2 * rank, 2 * rows), 1) // SUB
    ).astype(jnp.bfloat16)
    same_column = (
        lax.broadcasted_iota(jnp.int32, (2 * rows, 2 * rows), 0) % SUB
        == lax.broadcasted_iota(jnp.int32, (2 * rows, 2 * rows), 1) % SUB
    )

    def take_weights(slot, level, side):
        mixer = jnp.concatenate([mixers[level, side, side], mixers[level, side, 1 - side]], axis=1)
        parts = [
            jnp.broadcast_to(part.astype(jnp.float32)[:, None, :], (rank, SUB, 2 * rank)).reshape(rows, 2 * rank)
            for part in split(mixer)
        ]
        tall = jnp.concatenate(parts, axis=0).astype(jnp.bfloat16)
        wide_values = jnp.dot(tall, spread, preferred_element_type=jnp.float32)
        weights[slot] = jnp.where(same_column, wide_values, 0.0).astype(jnp.bfloat16)

    for level in (4, 5):
        take_cosines(level)
    for p in (2, 1, 3):
        cos_copy(p).start()
    z_cos[here] = cosines[:, here, 4:6]
    take_cosines(0)
    take_weights(0, 0, narrow % 2)

    def pair(ref, k, first, second):
        return jnp.concatenate([ref[k, first].reshape(rows, WIDTH), ref[k, second].reshape(rows, WIDTH)], axis=1)

    def put(ref, k, first, second, value):
        ref[k, first] = value[:, :WIDTH].reshape(rank, SUB, WIDTH)
        ref[k, second] = value[:, WIDTH:].reshape(rank, SUB, WIDTH)

    def angles(k, level, half):
        part = k % SPLITS
        return jnp.concatenate([cosines[part, 2 * half, level], cosines[part, 2 * half + 1, level]], axis=1)

    def level_0(k):
        for q in range(4):
            core_copy(k, q).wait()
            load(k, q).wait()
        for half in range(2):
            at = (2 * half, 2 * half + 1)
            value = mixed(weights.at[0], pair(a, k, *at), pair(c_core, k, *at))
            put(b, k, *at, scaled(value, angles(k, 0, half)))
        y_copy(k).start()

    def levels_1_2(k):
        y_copy(k).wait_recv()
        between = []
        for half in range(2):
            at = (2 * half, 2 * half + 1)
            value = mixed(weights.at[1], pair(b, k, *at), pair(c_y, k, *at))
            between.append(scaled(value, angles(k, 1, half)))
        for half in range(2):
            value = mixed(weights.at[2 + half], between[half], between[1 - half])
            put(a, k, 2 * half, 2 * half + 1, scaled(value, angles(k, 2, half)))
        x_copy(k).start()

    def level_3(k):
        x_copy(k).wait_recv()
        y_copy(k).wait_send()
        for half in range(2):
            at = (2 * half, 2 * half + 1)
            value = mixed(weights.at[4], pair(a, k, *at), pair(c_x, k, *at))
            put(b, k, *at, scaled(value, angles(k, 3, half)))
        for p in (2, 1, 3):
            z_copy(k, p).start()
        c_z[k, here] = b[k, here]

    def levels_4_5(k):
        part = k % SPLITS
        for p in (1, 2, 3):
            z_copy(k, p).wait_recv()
        x_copy(k).wait_send()
        even, odd = pair(c_z, k, 0, 2), pair(c_z, k, 1, 3)

        def z_angles(level, first, second):
            return jnp.concatenate([z_cos[first, part, level], z_cos[second, part, level]], axis=1)

        even, odd = (
            scaled(mixed(weights.at[5], even, odd), z_angles(0, 0, 2)),
            scaled(mixed(weights.at[6], odd, even), z_angles(0, 1, 3)),
        )
        low = jnp.concatenate([even[:, :WIDTH], odd[:, :WIDTH]], axis=1)
        high = jnp.concatenate([even[:, WIDTH:], odd[:, WIDTH:]], axis=1)
        put(a, k, 0, 1, scaled(mixed(weights.at[7], low, high), z_angles(1, 0, 1)))
        put(a, k, 2, 3, scaled(mixed(weights.at[8], high, low), z_angles(1, 2, 3)))
        for p in (2, 1, 3):
            back_copy(k, p).start()
        keep_copy(k).start()

    ahead = 2
    level_0(0)
    take_cosines(1)
    take_weights(1, 1, narrow // 4)
    level_0(1)
    take_cosines(2)
    take_cosines(3)
    for slot, level, side in ((2, 2, 0), (3, 2, 1), (4, 3, wide // 2 % 2), (5, 4, 0), (6, 4, 1), (7, 5, 0), (8, 5, 1)):
        take_weights(slot, level, side)
    for p in (1, 2, 3):
        cos_copy(p).wait()

    def tick(t, carry):
        pl.when(t < chunks)(lambda: levels_1_2(t))
        pl.when(t + ahead < chunks)(lambda: level_0(t + ahead))
        pl.when(jnp.logical_and(t >= 1, t < chunks + 1))(lambda: level_3(t - 1))
        pl.when(jnp.logical_and(t >= 2, t < chunks + 2))(lambda: levels_4_5(t - 2))
        return carry

    lax.fori_loop(0, chunks + 2, tick, 0)

    def drain(k, carry):
        for p in (1, 2, 3):
            z_copy(k, p).wait_send()
            back_copy(k, p).wait()
        keep_copy(k).wait()
        return carry

    lax.fori_loop(0, chunks, drain, 0)


def on_device(coeffs, phases, mixers):
    rank, columns, blocks = coeffs.shape
    levels = phases.shape[0]
    chunks = columns // SUB * SPLITS
    piece = pltpu.VMEM((chunks, 4, rank, SUB, WIDTH), jnp.float32)
    dma = pltpu.SemaphoreType.DMA
    any_space = pl.BlockSpec(memory_space=pl.ANY)
    vmem = pl.BlockSpec(memory_space=pltpu.VMEM)
    return pl.pallas_call(
        functools.partial(kernel, chunks, rank),
        out_shape=jax.ShapeDtypeStruct(coeffs.shape, coeffs.dtype),
        in_specs=[any_space, vmem, vmem],
        out_specs=any_space,
        scratch_shapes=[
            piece, piece, piece, piece, piece, piece,
            pltpu.VMEM((9, 2 * rank * SUB, 2 * rank * SUB), jnp.bfloat16),
            pltpu.VMEM((SPLITS, 4, levels, rank, WIDTH), jnp.float32),
            pltpu.VMEM((4, SPLITS, 2, rank, WIDTH), jnp.float32),
            dma((chunks, 4)), dma((chunks, 4)), dma((chunks, 4)),
            dma((chunks,)), dma((chunks,)), dma((chunks,)), dma((chunks,)),
            dma((chunks, 3)), dma((chunks, 3)), dma((chunks, 3)), dma((chunks, 3)),
            dma((chunks,)), dma((3,)), dma((3,)),
        ],
        compiler_params=pltpu.CompilerParams(
            collective_id=0, has_side_effects=True, vmem_limit_bytes=60 * 2**20
        ),
    )(coeffs, phases, mixers)


def solution(mesh):
    placed = (P(None, None, ("wide", "narrow")), P(None, None, ("wide", "narrow")), P())
    return jax.shard_map(
        on_device,
        mesh=mesh,
        in_specs=placed,
        out_specs=P(None, None, ("wide", "narrow")),
        check_vma=False,
    )
```

```python
import functools

import jax
import jax.numpy as jnp
from jax import lax
from jax.experimental import pallas as pl
from jax.experimental.pallas import tpu as pltpu
from jax.sharding import PartitionSpec as P

MESH = pl.DeviceIdType.MESH
SUB = 8
WIDTH = 128
AHEAD = 3
LAG_X = 2
LAG_Z = 4
FETCH = 4
ORDER = (2, 1, 3)


def split(x):
    high = x.astype(jnp.bfloat16)
    return high, (x - high.astype(jnp.float32)).astype(jnp.bfloat16)


def cosine(angle):
    half = 0.5 * angle
    square = half * half
    series = jnp.full_like(square, 1.0)
    for n in (12, 10, 8, 6, 4, 2):
        series = 1.0 - series * square * (1.0 / (n * (n + 1)))
    sine = half * series
    return 1.0 - 2.0 * sine * sine


def mixed(w, own, other):
    rows = own.shape[0]
    own_high, own_low = split(own)
    other_high, other_low = split(other)
    high = jnp.concatenate([own_high, other_high], axis=0)
    low = jnp.concatenate([own_low, other_low], axis=0)
    both = jnp.dot(w[...], high, preferred_element_type=jnp.float32)
    rest = jnp.dot(w[:rows], low, preferred_element_type=jnp.float32)
    return both[:rows] + (both[rows:] + rest)


def scaled(value, angle):
    rank, width = angle.shape
    return (value.reshape(rank, SUB, width) * angle[:, None, :]).reshape(rank * SUB, width)


def kernel(
    units, rank, coeffs, phases_in, mixers_in, out, a, b, c_core, c_y, c_x, c_z, phases, mixers, weights, cosines,
    z_cos, small_sem, load_sem, core_send, core_recv, y_send, y_recv, x_send, x_recv, z_send, z_recv,
    back_send, back_recv, keep_sem, cos_send, cos_recv,
):
    wide, narrow = lax.axis_index("wide"), lax.axis_index("narrow")
    here, column = wide // 4, wide % 4
    core_peer, y_peer, x_peer = (wide, narrow ^ 1), (wide, narrow ^ 4), (wide ^ 2, narrow)
    half_lanes = coeffs.shape[2] // 2
    rows = rank * SUB

    def z_device(there):
        return there * 4 + column, narrow

    barrier = pltpu.get_barrier_semaphore()
    peers = [core_peer, y_peer, x_peer, *(z_device(here ^ p) for p in ORDER)]
    for peer in peers:
        pl.semaphore_signal(barrier, inc=1, device_id=peer, device_id_type=MESH)

    def window(ref, group, half, tile):
        columns = pl.ds(pl.multiple_of(group * SUB, SUB), SUB)
        return ref.at[:, columns, pl.ds(pl.multiple_of(half * half_lanes + tile * WIDTH, WIDTH), WIDTH)]

    def remote(src, dst, send, recv, peer):
        return pltpu.make_async_remote_copy(src, dst, send, recv, device_id=peer, device_id_type=MESH)

    def load(k, half):
        return pltpu.make_async_copy(window(coeffs, k // 4, half, k % 4), a.at[k, half], load_sem.at[k, half])

    def core_copy(k, half):
        src = window(coeffs, k // 4, half, k % 4)
        return remote(src, c_core.at[k, half], core_send.at[k, half], core_recv.at[k, half], core_peer)

    def y_copy(k):
        return remote(b.at[k], c_y.at[k], y_send.at[k], y_recv.at[k], y_peer)

    def x_copy(k):
        return remote(a.at[k], c_x.at[k], x_send.at[k], x_recv.at[k], x_peer)

    def z_copy(k, half):
        there = 2 * half + k % 2
        return remote(b.at[k, half], c_z.at[k // 2, here], z_send.at[k, half], z_recv.at[k // 2, here], z_device(there))

    def z_arrival(s, there):
        return remote(b.at[2 * s, 0], c_z.at[s, there], z_send.at[2 * s, 0], z_recv.at[s, there], z_device(there))

    def back_copy(s, p):
        there = here ^ p
        src = a.at[2 * s + there // 2, there % 2]
        dst = window(out, s // 2, here // 2, 2 * (s % 2) + here % 2)
        return remote(src, dst, back_send.at[s, p - 1], back_recv.at[s, p - 1], z_device(there))

    def keep_copy(s):
        src = a.at[2 * s + here // 2, here % 2]
        return pltpu.make_async_copy(src, window(out, s // 2, here // 2, 2 * (s % 2) + here % 2), keep_sem.at[s])

    def cos_copy(p):
        there = here ^ p
        src = cosines.at[:, there % 2, there // 2, pl.ds(4, 2)]
        return remote(src, z_cos.at[here], cos_send.at[p - 1], cos_recv.at[p - 1], z_device(there))

    load_phases = pltpu.make_async_copy(phases_in, phases, small_sem.at[0])
    load_mixers = pltpu.make_async_copy(mixers_in, mixers, small_sem.at[1])
    load_mixers.start()
    load_phases.start()

    def fetch_own(k):
        for half in range(2):
            load(k, half).start()

    def fetch_core(k):
        for half in range(2):
            core_copy(k, half).start()

    for k in range(FETCH):
        fetch_own(k)

    def take_cosines(level):
        value = cosine(phases[level])
        for tile in range(4):
            for half in range(2):
                start = half * half_lanes + tile * WIDTH
                cosines[tile // 2, tile % 2, half, level] = value[:, start : start + WIDTH]

    spread = (
        lax.broadcasted_iota(jnp.int32, (2 * rank, 2 * rows), 0)
        == lax.broadcasted_iota(jnp.int32, (2 * rank, 2 * rows), 1) // SUB
    ).astype(jnp.bfloat16)
    same_column = (
        lax.broadcasted_iota(jnp.int32, (2 * rows, 2 * rows), 0) % SUB
        == lax.broadcasted_iota(jnp.int32, (2 * rows, 2 * rows), 1) % SUB
    )

    def take_weights(slot, level, side):
        mixer = jnp.concatenate([mixers[level, side, side], mixers[level, side, 1 - side]], axis=1)
        parts = [
            jnp.broadcast_to(part.astype(jnp.float32)[:, None, :], (rank, SUB, 2 * rank)).reshape(rows, 2 * rank)
            for part in split(mixer)
        ]
        tall = jnp.concatenate(parts, axis=0).astype(jnp.bfloat16)
        wide_values = jnp.dot(tall, spread, preferred_element_type=jnp.float32)
        weights[slot] = jnp.where(same_column, wide_values, 0.0).astype(jnp.bfloat16)

    load_mixers.wait()
    take_weights(0, 0, narrow % 2)
    load_phases.wait()
    take_cosines(0)
    pl.semaphore_wait(barrier, len(peers))
    for k in range(FETCH):
        fetch_core(k)
    take_weights(1, 1, narrow // 4)

    def both(ref, k):
        return jnp.concatenate([ref[k, 0].reshape(rows, WIDTH), ref[k, 1].reshape(rows, WIDTH)], axis=1)

    def put(ref, k, value):
        ref[k, 0] = value[:, :WIDTH].reshape(rank, SUB, WIDTH)
        ref[k, 1] = value[:, WIDTH:].reshape(rank, SUB, WIDTH)

    def angle(k, level, half):
        return cosines[k % 4 // 2, k % 2, half, level]

    def angles(k, level):
        return jnp.concatenate([angle(k, level, 0), angle(k, level, 1)], axis=1)

    def level_0(k):
        @pl.when(k + FETCH < units)
        def _():
            fetch_own(k + FETCH)
            fetch_core(k + FETCH)

        for half in range(2):
            core_copy(k, half).wait()
            load(k, half).wait()
        put(b, k, scaled(mixed(weights.at[0], both(a, k), both(c_core, k)), angles(k, 0)))
        y_copy(k).start()

    def levels_1_2(k):
        y_copy(k).wait_recv()
        value = scaled(mixed(weights.at[1], both(b, k), both(c_y, k)), angles(k, 1))
        low, high = value[:, :WIDTH], value[:, WIDTH:]
        a[k, 0] = scaled(mixed(weights.at[2], low, high), angle(k, 2, 0)).reshape(rank, SUB, WIDTH)
        a[k, 1] = scaled(mixed(weights.at[3], high, low), angle(k, 2, 1)).reshape(rank, SUB, WIDTH)
        x_copy(k).start()

    def level_3(k):
        x_copy(k).wait_recv()
        y_copy(k).wait_send()
        put(b, k, scaled(mixed(weights.at[4], both(a, k), both(c_x, k)), angles(k, 3)))
        for half in range(2):
            there = 2 * half + k % 2

            @pl.when(there != here)
            def _():
                z_copy(k, half).start()

            @pl.when(there == here)
            def _():
                c_z[k // 2, here] = b[k, half]

    def levels_4_5(s):
        for p in (1, 2, 3):
            z_arrival(s, here ^ p).wait_recv()
        x_copy(2 * s).wait_send()
        x_copy(2 * s + 1).wait_send()

        def z_pair(first, second):
            return jnp.concatenate([c_z[s, first].reshape(rows, WIDTH), c_z[s, second].reshape(rows, WIDTH)], axis=1)

        def z_angles(level, first, second):
            return jnp.concatenate([z_cos[first, s % 2, level], z_cos[second, s % 2, level]], axis=1)

        even, odd = z_pair(0, 2), z_pair(1, 3)
        even, odd = (
            scaled(mixed(weights.at[5], even, odd), z_angles(0, 0, 2)),
            scaled(mixed(weights.at[6], odd, even), z_angles(0, 1, 3)),
        )
        low = jnp.concatenate([even[:, :WIDTH], odd[:, :WIDTH]], axis=1)
        high = jnp.concatenate([even[:, WIDTH:], odd[:, WIDTH:]], axis=1)
        put(a, 2 * s, scaled(mixed(weights.at[7], low, high), z_angles(1, 0, 1)))
        put(a, 2 * s + 1, scaled(mixed(weights.at[8], high, low), z_angles(1, 2, 3)))
        for p in ORDER:
            back_copy(s, p).start()
        keep_copy(s).start()

    level_0(0)
    level_0(1)
    take_cosines(1)
    take_cosines(2)
    for slot, level, side in ((2, 2, 0), (3, 2, 1)):
        take_weights(slot, level, side)
    for level in (4, 5):
        take_cosines(level)
    for p in ORDER:
        cos_copy(p).start()
    z_cos[here] = cosines[:, here % 2, here // 2, 4:6]
    level_0(2)
    take_cosines(3)
    for slot, level, side in ((4, 3, wide // 2 % 2), (5, 4, 0), (6, 4, 1), (7, 5, 0), (8, 5, 1)):
        take_weights(slot, level, side)

    def tick(t, carry):
        levels_1_2(t)
        pl.when(t >= LAG_X)(lambda: level_3(t - LAG_X))
        pl.when(jnp.logical_and(t > LAG_Z, (t - LAG_Z) % 2 == 1))(lambda: levels_4_5((t - LAG_Z - 1) // 2))
        pl.when(t + AHEAD < units)(lambda: level_0(t + AHEAD))
        return carry

    def last(i, carry):
        level_3(units - 2 + i)
        levels_4_5(units // 2 - 2 + i)
        return carry

    lax.fori_loop(0, 4, tick, 0)
    for p in (1, 2, 3):
        cos_copy(p).wait()
    lax.fori_loop(4, units, tick, 0)
    lax.fori_loop(0, 2, last, 0)

    def drain(s, carry):
        for k in (2 * s, 2 * s + 1):
            for half in range(2):
                pl.when(2 * half + k % 2 != here)(z_copy(k, half).wait_send)
        for p in (1, 2, 3):
            back_copy(s, p).wait()
        keep_copy(s).wait()
        return carry

    lax.fori_loop(0, units // 2, drain, 0)


def on_device(coeffs, phases, mixers):
    rank, columns, blocks = coeffs.shape
    levels = phases.shape[0]
    units = columns // SUB * (blocks // (2 * WIDTH))

    piece = pltpu.VMEM((units, 2, rank, SUB, WIDTH), jnp.float32)
    dma = pltpu.SemaphoreType.DMA
    any_space = pl.BlockSpec(memory_space=pl.ANY)
    vmem = pl.BlockSpec(memory_space=pltpu.VMEM)
    return pl.pallas_call(
        functools.partial(kernel, units, rank),
        out_shape=pltpu.VMEM(coeffs.shape, coeffs.dtype),
        in_specs=[any_space, any_space, any_space],
        out_specs=vmem,
        scratch_shapes=[
            piece, piece, piece, piece, piece,
            pltpu.VMEM((units // 2, 4, rank, SUB, WIDTH), jnp.float32),
            pltpu.VMEM(phases.shape, jnp.float32),
            pltpu.VMEM(mixers.shape, jnp.float32),
            pltpu.VMEM((9, 2 * rank * SUB, 2 * rank * SUB), jnp.bfloat16),
            pltpu.VMEM((2, 2, 2, levels, rank, WIDTH), jnp.float32),
            pltpu.VMEM((4, 2, 2, rank, WIDTH), jnp.float32),
            dma((2,)), dma((units, 2)), dma((units, 2)), dma((units, 2)),
            dma((units,)), dma((units,)), dma((units,)), dma((units,)),
            dma((units, 2)), dma((units // 2, 4)), dma((units // 2, 3)), dma((units // 2, 3)),
            dma((units // 2,)), dma((3,)), dma((3,)),
        ],
        compiler_params=pltpu.CompilerParams(
            collective_id=0, has_side_effects=True, vmem_limit_bytes=48 * 2**20
        ),
    )(coeffs, phases, mixers)


def solution(mesh):
    placed = (P(None, None, ("wide", "narrow")), P(None, None, ("wide", "narrow")), P())
    return jax.shard_map(
        on_device,
        mesh=mesh,
        in_specs=placed,
        out_specs=P(None, None, ("wide", "narrow")),
        check_vma=False,
    )
```

```python
import functools

import jax
import jax.numpy as jnp
from jax import lax
from jax.experimental import pallas as pl
from jax.experimental.pallas import tpu as pltpu
from jax.sharding import PartitionSpec as P

MESH = pl.DeviceIdType.MESH
SUB = 8
WIDTH = 128
AHEAD = 3
LAG_X = 1
LAG_Z = 3
LAG_OUT = 5
FETCH = 4
ORDER = (2, 1, 3)
QUARTER = WIDTH // 2


def split(x):
    high = x.astype(jnp.bfloat16)
    return high, (x - high.astype(jnp.float32)).astype(jnp.bfloat16)


def cosine(angle):
    half = 0.5 * angle
    square = half * half
    series = jnp.full_like(square, 1.0)
    for n in (12, 10, 8, 6, 4, 2):
        series = 1.0 - series * square * (1.0 / (n * (n + 1)))
    sine = half * series
    return 1.0 - 2.0 * sine * sine


def mixed(w, own, other):
    rows = w.shape[0] // 2
    own_high, own_low = split(own)
    other_high, other_low = split(other)
    high = jnp.concatenate([own_high, other_high], axis=0)
    low = jnp.concatenate([own_low, other_low], axis=0)
    both = jnp.dot(w[...], high, preferred_element_type=jnp.float32)
    rest = jnp.dot(w[:rows], low, preferred_element_type=jnp.float32)
    return both[:rows] + (both[rows:] + rest)


def halves(first, second):
    lane = lax.broadcasted_iota(jnp.int32, first.shape, first.ndim - 1)
    near = lane < QUARTER
    turn = functools.partial(pltpu.roll, shift=QUARTER, axis=first.ndim - 1)
    return jnp.where(near, first, turn(second)), jnp.where(near, turn(first), second)


def scaled(value, angle):
    rank, width = angle.shape
    return (value.reshape(rank, SUB, width) * angle[:, None, :]).reshape(rank * SUB, width)


def kernel(
    units, rank, coeffs, phases_in, mixers_in, out, a, b, c_core, c_y, c_x, c_z, phases, mixers, weights, weights_two,
    cosines, z_cos, z_scale, small_sem, load_sem, core_send, core_recv, y_send, y_recv, x_send, x_recv, z_send, z_recv,
    back_send, back_recv, cos_send, cos_recv,
):
    wide, narrow = lax.axis_index("wide"), lax.axis_index("narrow")
    here, column = wide // 4, wide % 4
    core_peer, y_peer, x_peer = (wide, narrow ^ 1), (wide, narrow ^ 4), (wide ^ 2, narrow)
    half_lanes = coeffs.shape[2] // 2
    rows = rank * SUB

    def z_device(there):
        return there * 4 + column, narrow

    barrier = pltpu.get_barrier_semaphore()
    peers = [core_peer, y_peer, x_peer, *(z_device(here ^ p) for p in ORDER)]
    for peer in peers:
        pl.semaphore_signal(barrier, inc=1, device_id=peer, device_id_type=MESH)

    def window(ref, group, half, tile):
        columns = pl.ds(pl.multiple_of(group * SUB, SUB), SUB)
        return ref.at[:, columns, pl.ds(pl.multiple_of(half * half_lanes + tile * WIDTH, WIDTH), WIDTH)]

    def remote(src, dst, send, recv, peer):
        return pltpu.make_async_remote_copy(src, dst, send, recv, device_id=peer, device_id_type=MESH)

    def load(k, half):
        return pltpu.make_async_copy(window(coeffs, k // 4, half, k % 4), a.at[k, half], load_sem.at[k, half])

    def core_copy(k, half):
        src = window(coeffs, k // 4, half, k % 4)
        return remote(src, c_core.at[k, half], core_send.at[k, half], core_recv.at[k, half], core_peer)

    def y_copy(k):
        return remote(b.at[k], c_y.at[k], y_send.at[k], y_recv.at[k], y_peer)

    def x_copy(k):
        return remote(a.at[k], c_x.at[k], x_send.at[k], x_recv.at[k], x_peer)

    def piece(ref, k, there):
        return ref.at[k, there // 2, pl.ds(there % 2 * (rank // 2), rank // 2)]

    def z_copy(k, p):
        there = here ^ p
        src, dst = piece(b, k, there), piece(c_z, k, here)
        return remote(src, dst, z_send.at[k, p - 1], z_recv.at[k, p - 1], z_device(there))

    def back_copy(k, p):
        there = here ^ p
        src, dst = piece(a, k, there), piece(c_core, k, here)
        return remote(src, dst, back_send.at[k, p - 1], back_recv.at[k, p - 1], z_device(there))

    def cos_copy(p):
        there = here ^ p
        src = cosines.at[:, :, there // 2, pl.ds(4, 2)]
        return remote(src, z_cos.at[here], cos_send.at[p - 1], cos_recv.at[p - 1], z_device(there))

    load_phases = pltpu.make_async_copy(phases_in, phases, small_sem.at[0])
    load_mixers = pltpu.make_async_copy(mixers_in, mixers, small_sem.at[1])
    load_mixers.start()
    load_phases.start()

    def fetch_own(k):
        for half in range(2):
            load(k, half).start()

    def fetch_core(k):
        for half in range(2):
            core_copy(k, half).start()

    for k in range(FETCH):
        fetch_own(k)

    def take_cosines(level):
        value = cosine(phases[level])
        for tile in range(4):
            for half in range(2):
                start = half * half_lanes + tile * WIDTH
                cosines[tile // 2, tile % 2, half, level] = value[:, start : start + WIDTH]

    spread = (
        lax.broadcasted_iota(jnp.int32, (2 * rank, 2 * rows), 0)
        == lax.broadcasted_iota(jnp.int32, (2 * rank, 2 * rows), 1) // SUB
    ).astype(jnp.bfloat16)
    same_column = (
        lax.broadcasted_iota(jnp.int32, (2 * rows, 2 * rows), 0) % SUB
        == lax.broadcasted_iota(jnp.int32, (2 * rows, 2 * rows), 1) % SUB
    )

    def take_weights(slot, level, side):
        mixer = jnp.concatenate([mixers[level, side, side], mixers[level, side, 1 - side]], axis=1)
        parts = [
            jnp.broadcast_to(part.astype(jnp.float32)[:, None, :], (rank, SUB, 2 * rank)).reshape(rows, 2 * rank)
            for part in split(mixer)
        ]
        tall = jnp.concatenate(parts, axis=0).astype(jnp.bfloat16)
        wide_values = jnp.dot(tall, spread, preferred_element_type=jnp.float32)
        weights[slot] = jnp.where(same_column, wide_values, 0.0).astype(jnp.bfloat16)

    def take_weights_two(slot, level):
        mixer = jnp.concatenate(
            [jnp.concatenate([mixers[level, side, 0], mixers[level, side, 1]], axis=1) for side in range(2)], axis=0
        )
        for at, part in enumerate(split(mixer)):
            tall = jnp.broadcast_to(part.astype(jnp.float32)[:, None, :], (2 * rank, SUB, 2 * rank))
            tall = tall.reshape(2 * rows, 2 * rank).astype(jnp.bfloat16)
            wide_values = jnp.dot(tall, spread, preferred_element_type=jnp.float32)
            values = jnp.where(same_column, wide_values, 0.0).astype(jnp.bfloat16)
            weights_two[slot, at * 2 * rows : (at + 1) * 2 * rows] = values

    load_mixers.wait()
    take_weights(0, 0, narrow % 2)
    load_phases.wait()
    take_cosines(0)
    pl.semaphore_wait(barrier, len(peers))
    for k in range(FETCH):
        fetch_core(k)
    take_weights(1, 1, narrow // 4)

    def both(ref, k):
        return jnp.concatenate([ref[k, 0].reshape(rows, WIDTH), ref[k, 1].reshape(rows, WIDTH)], axis=1)

    def put(ref, k, value):
        ref[k, 0] = value[:, :WIDTH].reshape(rank, SUB, WIDTH)
        ref[k, 1] = value[:, WIDTH:].reshape(rank, SUB, WIDTH)

    def angle(k, level, half):
        return cosines[k % 4 // 2, k % 2, half, level]

    def angles(k, level):
        return jnp.concatenate([angle(k, level, 0), angle(k, level, 1)], axis=1)

    def level_0(k):
        @pl.when(k + FETCH < units)
        def _():
            fetch_own(k + FETCH)
            fetch_core(k + FETCH)

        for half in range(2):
            core_copy(k, half).wait()
            load(k, half).wait()
        put(b, k, scaled(mixed(weights.at[0], both(a, k), both(c_core, k)), angles(k, 0)))
        y_copy(k).start()

    def levels_1_2(k):
        y_copy(k).wait_recv()
        value = scaled(mixed(weights.at[1], both(b, k), both(c_y, k)), angles(k, 1))
        value = mixed(weights_two.at[0], value[:, :WIDTH], value[:, WIDTH:])
        for half in range(2):
            part = scaled(value[half * rows : (half + 1) * rows], angle(k, 2, half))
            a[k, half] = part.reshape(rank, SUB, WIDTH)
        x_copy(k).start()

    def put_pieces(ref, k, half, tile):
        first, second = halves(tile[: rank // 2], tile[rank // 2 :])
        ref[k, half, : rank // 2] = first
        ref[k, half, rank // 2 :] = second

    def join(first, second):
        return jnp.concatenate(halves(first, second), axis=0)

    def level_3(k):
        x_copy(k).wait_recv()
        y_copy(k).wait_send()
        value = scaled(mixed(weights.at[2], both(a, k), both(c_x, k)), angles(k, 3))
        for half in range(2):
            put_pieces(b, k, half, value[:, half * WIDTH : (half + 1) * WIDTH].reshape(rank, SUB, WIDTH))
        for p in ORDER:
            z_copy(k, p).start()
        piece(c_z, k, here)[...] = piece(b, k, here)[...]

    def levels_4_5(k):
        for p in (1, 2, 3):
            z_copy(k, p).wait_recv()
        x_copy(k).wait_send()

        def z_piece(there):
            return c_z[k, there // 2, there % 2 * (rank // 2) : (there % 2 + 1) * (rank // 2)]

        def scale(n):
            return z_scale[k % 4 // 2, k % 2, n]

        even, odd = join(z_piece(0), z_piece(2)), join(z_piece(1), z_piece(3))
        value = mixed(weights_two.at[1], even.reshape(rows, WIDTH), odd.reshape(rows, WIDTH))
        low, high = halves(scaled(value[:rows], scale(0)), scaled(value[rows:], scale(1)))
        value = mixed(weights_two.at[2], low, high)
        for half in range(2):
            tile = scaled(value[half * rows : (half + 1) * rows], scale(2 + half))
            put_pieces(a, k, half, tile.reshape(rank, SUB, WIDTH))
        for p in ORDER:
            back_copy(k, p).start()
        piece(c_core, k, here)[...] = piece(a, k, here)[...]

    def result(k):
        for p in (1, 2, 3):
            back_copy(k, p).wait()
            z_copy(k, p).wait_send()
        for half in range(2):
            tile = join(c_core[k, half, : rank // 2], c_core[k, half, rank // 2 :])
            window(out, k // 4, half, k % 4)[...] = tile

    def take_z_scale():
        side = here % 2
        for tile in range(4):
            for level, pairs in enumerate((((0, 2), (1, 3)), ((0, 1), (2, 3)))):
                for at, pair in enumerate(pairs):
                    first, second = (z_cos[there, tile // 2, tile % 2, level] for there in pair)
                    near, far = halves(first, second)
                    z_scale[tile // 2, tile % 2, 2 * level + at] = jnp.where(side == 0, near, far)

    level_0(0)
    level_0(1)
    take_cosines(1)
    take_cosines(2)
    take_weights_two(0, 2)
    for level in (4, 5):
        take_cosines(level)
    for p in ORDER:
        cos_copy(p).start()
    z_cos[here] = cosines[:, :, here // 2, 4:6]
    level_0(2)
    take_cosines(3)
    take_weights(2, 3, wide // 2 % 2)
    take_weights_two(1, 4)
    take_weights_two(2, 5)

    def finish(t):
        pl.when(t >= LAG_Z)(lambda: levels_4_5(t - LAG_Z))
        pl.when(t >= LAG_OUT)(lambda: result(t - LAG_OUT))

    def tick(t, carry):
        levels_1_2(t)
        finish(t)
        pl.when(t + AHEAD < units)(lambda: level_0(t + AHEAD))
        pl.when(t >= LAG_X)(lambda: level_3(t - LAG_X))
        return carry

    def last(t, carry):
        finish(t)
        pl.when(t < units + LAG_X)(lambda: level_3(t - LAG_X))
        return carry

    def very_last(k, carry):
        result(k)
        return carry

    lax.fori_loop(0, LAG_Z, tick, 0)
    for p in (1, 2, 3):
        cos_copy(p).wait()
    take_z_scale()
    lax.fori_loop(LAG_Z, units, tick, 0)
    lax.fori_loop(units, units + LAG_Z, last, 0)
    lax.fori_loop(units + LAG_Z - LAG_OUT, units, very_last, 0)


def on_device(coeffs, phases, mixers):
    rank, columns, blocks = coeffs.shape
    levels = phases.shape[0]
    units = columns // SUB * (blocks // (2 * WIDTH))

    piece = pltpu.VMEM((units, 2, rank, SUB, WIDTH), jnp.float32)
    dma = pltpu.SemaphoreType.DMA
    any_space = pl.BlockSpec(memory_space=pl.ANY)
    vmem = pl.BlockSpec(memory_space=pltpu.VMEM)
    return pl.pallas_call(
        functools.partial(kernel, units, rank),
        out_shape=pltpu.VMEM(coeffs.shape, coeffs.dtype),
        in_specs=[any_space, any_space, any_space],
        out_specs=vmem,
        scratch_shapes=[
            piece, piece, piece, piece, piece, piece,
            pltpu.VMEM(phases.shape, jnp.float32),
            pltpu.VMEM(mixers.shape, jnp.float32),
            pltpu.VMEM((3, 2 * rank * SUB, 2 * rank * SUB), jnp.bfloat16),
            pltpu.VMEM((3, 4 * rank * SUB, 2 * rank * SUB), jnp.bfloat16),
            pltpu.VMEM((2, 2, 2, levels, rank, WIDTH), jnp.float32),
            pltpu.VMEM((4, 2, 2, 2, rank, WIDTH), jnp.float32),
            pltpu.VMEM((2, 2, 4, rank, WIDTH), jnp.float32),
            dma((2,)), dma((units, 2)), dma((units, 2)), dma((units, 2)),
            dma((units,)), dma((units,)), dma((units,)), dma((units,)),
            dma((units, 3)), dma((units, 3)), dma((units, 3)), dma((units, 3)),
            dma((3,)), dma((3,)),
        ],
        compiler_params=pltpu.CompilerParams(
            collective_id=0, has_side_effects=True, vmem_limit_bytes=48 * 2**20
        ),
    )(coeffs, phases, mixers)


def solution(mesh):
    placed = (P(None, None, ("wide", "narrow")), P(None, None, ("wide", "narrow")), P())
    return jax.shard_map(
        on_device,
        mesh=mesh,
        in_specs=placed,
        out_specs=P(None, None, ("wide", "narrow")),
        check_vma=False,
    )
```

```python
import functools

import jax
import jax.numpy as jnp
from jax import lax
from jax.experimental import pallas as pl
from jax.experimental.pallas import tpu as pltpu
from jax.sharding import PartitionSpec as P

MESH = pl.DeviceIdType.MESH
SUB = 8
WIDTH = 128
AHEAD = 3
LAG_X = 1
LAG_Z = 3
LAG_OUT = 5
FETCH = 8
SHARE = 4
ORDER = (2, 1, 3)
QUARTER = WIDTH // 2


def split(x):
    high = x.astype(jnp.bfloat16)
    return high, (x - high.astype(jnp.float32)).astype(jnp.bfloat16)


def cosine(angle):
    half = 0.5 * angle
    square = half * half
    series = jnp.full_like(square, 1.0)
    for n in (12, 10, 8, 6, 4, 2):
        series = 1.0 - series * square * (1.0 / (n * (n + 1)))
    sine = half * series
    return 1.0 - 2.0 * sine * sine


def mixed(w, own, other):
    rows = w.shape[0] // 2
    own_high, own_low = split(own)
    other_high, other_low = split(other)
    high = jnp.concatenate([own_high, other_high], axis=0)
    low = jnp.concatenate([own_low, other_low], axis=0)
    both = jnp.dot(w[...], high, preferred_element_type=jnp.float32)
    rest = jnp.dot(w[:rows], low, preferred_element_type=jnp.float32)
    return both[:rows] + (both[rows:] + rest)


def halves(first, second):
    lane = lax.broadcasted_iota(jnp.int32, first.shape, first.ndim - 1)
    near = lane < QUARTER
    turn = functools.partial(pltpu.roll, shift=QUARTER, axis=first.ndim - 1)
    return jnp.where(near, first, turn(second)), jnp.where(near, turn(first), second)


def scaled(value, angle):
    rank, width = angle.shape
    return (value.reshape(rank, SUB, width) * angle[:, None, :]).reshape(rank * SUB, width)


def kernel(
    units, rank, coeffs, phases_in, mixers_in, out, a, b, c_core, c_y, c_x, c_z, phases, mixers, weights, weights_two,
    cosines, z_cos, z_scale, small_sem, load_sem, core_send, core_recv, y_send, y_recv, x_send, x_recv, z_send, z_recv,
    back_send, back_recv, cos_send, cos_recv,
):
    wide, narrow = lax.axis_index("wide"), lax.axis_index("narrow")
    here, column = wide // 4, wide % 4
    core_peer, y_peer, x_peer = (wide, narrow ^ 1), (wide, narrow ^ 4), (wide ^ 2, narrow)
    half_lanes = coeffs.shape[2] // 2
    rows = rank * SUB

    def z_device(there):
        return there * 4 + column, narrow

    barrier = pltpu.get_barrier_semaphore()
    peers = [core_peer, y_peer, x_peer, *(z_device(here ^ p) for p in ORDER)]
    for peer in peers:
        pl.semaphore_signal(barrier, inc=1, device_id=peer, device_id_type=MESH)

    def window(ref, group, half, tile):
        columns = pl.ds(pl.multiple_of(group * SUB, SUB), SUB)
        return ref.at[:, columns, pl.ds(pl.multiple_of(half * half_lanes + tile * WIDTH, WIDTH), WIDTH)]

    def remote(src, dst, send, recv, peer):
        return pltpu.make_async_remote_copy(src, dst, send, recv, device_id=peer, device_id_type=MESH)

    def load(k, half):
        return pltpu.make_async_copy(window(coeffs, k // 4, half, k % 4), a.at[k, half], load_sem.at[k, half])

    def core_copy(k):
        return remote(a.at[k], c_core.at[k], core_send.at[k], core_recv.at[k], core_peer)

    def y_copy(k):
        return remote(b.at[k], c_y.at[k], y_send.at[k], y_recv.at[k], y_peer)

    def x_copy(k):
        return remote(a.at[k], c_x.at[k], x_send.at[k], x_recv.at[k], x_peer)

    def piece(ref, k, there):
        return ref.at[k, there // 2, pl.ds(there % 2 * (rank // 2), rank // 2)]

    def z_copy(k, p):
        there = here ^ p
        src, dst = piece(b, k, there), piece(c_z, k, here)
        return remote(src, dst, z_send.at[k, p - 1], z_recv.at[k, p - 1], z_device(there))

    def back_copy(k, p):
        there = here ^ p
        src, dst = piece(a, k, there), piece(c_core, k, here)
        return remote(src, dst, back_send.at[k, p - 1], back_recv.at[k, p - 1], z_device(there))

    def cos_copy(p):
        there = here ^ p
        src = cosines.at[:, :, there // 2, pl.ds(4, 2)]
        return remote(src, z_cos.at[here], cos_send.at[p - 1], cos_recv.at[p - 1], z_device(there))

    load_phases = pltpu.make_async_copy(phases_in, phases, small_sem.at[0])
    load_mixers = pltpu.make_async_copy(mixers_in, mixers, small_sem.at[1])
    load_mixers.start()
    load_phases.start()

    def fetch_own(k):
        for half in range(2):
            load(k, half).start()

    def share(k):
        for half in range(2):
            load(k, half).wait()
        core_copy(k).start()

    for k in range(FETCH):
        fetch_own(k)
    pl.semaphore_wait(barrier, len(peers))
    for k in range(SHARE):
        share(k)

    def take_cosines(level):
        value = cosine(phases[level])
        for tile in range(4):
            for half in range(2):
                start = half * half_lanes + tile * WIDTH
                cosines[tile // 2, tile % 2, half, level] = value[:, start : start + WIDTH]

    spread = (
        lax.broadcasted_iota(jnp.int32, (2 * rank, 2 * rows), 0)
        == lax.broadcasted_iota(jnp.int32, (2 * rank, 2 * rows), 1) // SUB
    ).astype(jnp.bfloat16)
    same_column = (
        lax.broadcasted_iota(jnp.int32, (2 * rows, 2 * rows), 0) % SUB
        == lax.broadcasted_iota(jnp.int32, (2 * rows, 2 * rows), 1) % SUB
    )

    def take_weights(slot, level, side):
        mixer = jnp.concatenate([mixers[level, side, side], mixers[level, side, 1 - side]], axis=1)
        parts = [
            jnp.broadcast_to(part.astype(jnp.float32)[:, None, :], (rank, SUB, 2 * rank)).reshape(rows, 2 * rank)
            for part in split(mixer)
        ]
        tall = jnp.concatenate(parts, axis=0).astype(jnp.bfloat16)
        wide_values = jnp.dot(tall, spread, preferred_element_type=jnp.float32)
        weights[slot] = jnp.where(same_column, wide_values, 0.0).astype(jnp.bfloat16)

    def take_weights_two(slot, level):
        mixer = jnp.concatenate(
            [jnp.concatenate([mixers[level, side, 0], mixers[level, side, 1]], axis=1) for side in range(2)], axis=0
        )
        for at, part in enumerate(split(mixer)):
            tall = jnp.broadcast_to(part.astype(jnp.float32)[:, None, :], (2 * rank, SUB, 2 * rank))
            tall = tall.reshape(2 * rows, 2 * rank).astype(jnp.bfloat16)
            wide_values = jnp.dot(tall, spread, preferred_element_type=jnp.float32)
            values = jnp.where(same_column, wide_values, 0.0).astype(jnp.bfloat16)
            weights_two[slot, at * 2 * rows : (at + 1) * 2 * rows] = values

    load_mixers.wait()
    take_weights(0, 0, narrow % 2)
    load_phases.wait()
    take_cosines(0)

    def both(ref, k):
        return jnp.concatenate([ref[k, 0].reshape(rows, WIDTH), ref[k, 1].reshape(rows, WIDTH)], axis=1)

    def put(ref, k, value):
        ref[k, 0] = value[:, :WIDTH].reshape(rank, SUB, WIDTH)
        ref[k, 1] = value[:, WIDTH:].reshape(rank, SUB, WIDTH)

    def angle(k, level, half):
        return cosines[k % 4 // 2, k % 2, half, level]

    def angles(k, level):
        return jnp.concatenate([angle(k, level, 0), angle(k, level, 1)], axis=1)

    def level_0(k):
        pl.when(k + FETCH < units)(lambda: fetch_own(k + FETCH))
        pl.when(k + SHARE < units)(lambda: share(k + SHARE))
        core_copy(k).wait()
        put(b, k, scaled(mixed(weights.at[0], both(a, k), both(c_core, k)), angles(k, 0)))
        y_copy(k).start()

    def levels_1_2(k):
        y_copy(k).wait_recv()
        value = scaled(mixed(weights.at[1], both(b, k), both(c_y, k)), angles(k, 1))
        value = mixed(weights_two.at[0], value[:, :WIDTH], value[:, WIDTH:])
        for half in range(2):
            part = scaled(value[half * rows : (half + 1) * rows], angle(k, 2, half))
            a[k, half] = part.reshape(rank, SUB, WIDTH)
        x_copy(k).start()

    def put_pieces(ref, k, half, tile):
        first, second = halves(tile[: rank // 2], tile[rank // 2 :])
        ref[k, half, : rank // 2] = first
        ref[k, half, rank // 2 :] = second

    def join(first, second):
        return jnp.concatenate(halves(first, second), axis=0)

    def level_3(k):
        x_copy(k).wait_recv()
        y_copy(k).wait_send()
        value = scaled(mixed(weights.at[2], both(a, k), both(c_x, k)), angles(k, 3))
        for half in range(2):
            put_pieces(b, k, half, value[:, half * WIDTH : (half + 1) * WIDTH].reshape(rank, SUB, WIDTH))
        for p in ORDER:
            z_copy(k, p).start()
        piece(c_z, k, here)[...] = piece(b, k, here)[...]

    def levels_4_5(k):
        for p in (1, 2, 3):
            z_copy(k, p).wait_recv()
        x_copy(k).wait_send()

        def z_piece(there):
            return c_z[k, there // 2, there % 2 * (rank // 2) : (there % 2 + 1) * (rank // 2)]

        def scale(n):
            return z_scale[k % 4 // 2, k % 2, n]

        even, odd = join(z_piece(0), z_piece(2)), join(z_piece(1), z_piece(3))
        value = mixed(weights_two.at[1], even.reshape(rows, WIDTH), odd.reshape(rows, WIDTH))
        low, high = halves(scaled(value[:rows], scale(0)), scaled(value[rows:], scale(1)))
        value = mixed(weights_two.at[2], low, high)
        for half in range(2):
            tile = scaled(value[half * rows : (half + 1) * rows], scale(2 + half))
            put_pieces(a, k, half, tile.reshape(rank, SUB, WIDTH))
        for p in ORDER:
            back_copy(k, p).start()
        piece(c_core, k, here)[...] = piece(a, k, here)[...]

    def result(k):
        for p in (1, 2, 3):
            back_copy(k, p).wait()
            z_copy(k, p).wait_send()
        for half in range(2):
            tile = join(c_core[k, half, : rank // 2], c_core[k, half, rank // 2 :])
            window(out, k // 4, half, k % 4)[...] = tile

    def take_z_scale():
        side = here % 2
        for tile in range(4):
            for level, pairs in enumerate((((0, 2), (1, 3)), ((0, 1), (2, 3)))):
                for at, pair in enumerate(pairs):
                    first, second = (z_cos[there, tile // 2, tile % 2, level] for there in pair)
                    near, far = halves(first, second)
                    z_scale[tile // 2, tile % 2, 2 * level + at] = jnp.where(side == 0, near, far)

    level_0(0)
    take_weights(1, 1, narrow // 4)
    take_cosines(1)
    level_0(1)
    take_cosines(2)
    take_weights_two(0, 2)
    level_0(2)

    def before_level_3():
        take_cosines(3)
        take_weights(2, 3, wide // 2 % 2)
        for level in (4, 5):
            take_cosines(level)
        for p in ORDER:
            cos_copy(p).start()
        z_cos[here] = cosines[:, :, here // 2, 4:6]

    def before_level_5():
        take_weights_two(1, 4)
        take_weights_two(2, 5)
        for p in (1, 2, 3):
            cos_copy(p).wait()
        take_z_scale()

    def finish(t):
        pl.when(t >= LAG_Z)(lambda: levels_4_5(t - LAG_Z))
        pl.when(t >= LAG_OUT)(lambda: result(t - LAG_OUT))

    def tick(t, carry):
        levels_1_2(t)
        finish(t)
        pl.when(t + AHEAD < units)(lambda: level_0(t + AHEAD))
        pl.when(t >= LAG_X)(lambda: level_3(t - LAG_X))
        pl.when(t == 0)(before_level_3)
        pl.when(t == LAG_Z - 1)(before_level_5)
        return carry

    def last(t, carry):
        finish(t)
        pl.when(t < units + LAG_X)(lambda: level_3(t - LAG_X))
        return carry

    def very_last(k, carry):
        result(k)
        return carry

    lax.fori_loop(0, units, tick, 0)
    lax.fori_loop(units, units + LAG_Z, last, 0)
    lax.fori_loop(units + LAG_Z - LAG_OUT, units, very_last, 0)


def on_device(coeffs, phases, mixers):
    rank, columns, blocks = coeffs.shape
    levels = phases.shape[0]
    units = columns // SUB * (blocks // (2 * WIDTH))

    piece = pltpu.VMEM((units, 2, rank, SUB, WIDTH), jnp.float32)
    dma = pltpu.SemaphoreType.DMA
    any_space = pl.BlockSpec(memory_space=pl.ANY)
    vmem = pl.BlockSpec(memory_space=pltpu.VMEM)
    return pl.pallas_call(
        functools.partial(kernel, units, rank),
        out_shape=pltpu.VMEM(coeffs.shape, coeffs.dtype),
        in_specs=[any_space, any_space, any_space],
        out_specs=vmem,
        scratch_shapes=[
            piece, piece, piece, piece, piece, piece,
            pltpu.VMEM(phases.shape, jnp.float32),
            pltpu.VMEM(mixers.shape, jnp.float32),
            pltpu.VMEM((3, 2 * rank * SUB, 2 * rank * SUB), jnp.bfloat16),
            pltpu.VMEM((3, 4 * rank * SUB, 2 * rank * SUB), jnp.bfloat16),
            pltpu.VMEM((2, 2, 2, levels, rank, WIDTH), jnp.float32),
            pltpu.VMEM((4, 2, 2, 2, rank, WIDTH), jnp.float32),
            pltpu.VMEM((2, 2, 4, rank, WIDTH), jnp.float32),
            dma((2,)), dma((units, 2)), dma((units,)), dma((units,)),
            dma((units,)), dma((units,)), dma((units,)), dma((units,)),
            dma((units, 3)), dma((units, 3)), dma((units, 3)), dma((units, 3)),
            dma((3,)), dma((3,)),
        ],
        compiler_params=pltpu.CompilerParams(
            collective_id=0, has_side_effects=True, vmem_limit_bytes=48 * 2**20
        ),
    )(coeffs, phases, mixers)


def solution(mesh):
    placed = (P(None, None, ("wide", "narrow")), P(None, None, ("wide", "narrow")), P())
    return jax.shard_map(
        on_device,
        mesh=mesh,
        in_specs=placed,
        out_specs=P(None, None, ("wide", "narrow")),
        check_vma=False,
    )
```

```python
import functools

import jax
import jax.numpy as jnp
from jax import lax
from jax.experimental import pallas as pl
from jax.experimental.pallas import tpu as pltpu
from jax.sharding import PartitionSpec as P

MESH = pl.DeviceIdType.MESH
SUB = 8
WIDTH = 128
AHEAD = 3
LAG_X = 1
LAG_Z = 3
LAG_OUT = 5
FETCH = 8
SHARE = 4
ORDER = (2, 1, 3)
QUARTER = WIDTH // 2


def split(x):
    high = x.astype(jnp.bfloat16)
    return high, (x - high.astype(jnp.float32)).astype(jnp.bfloat16)


def cosine(angle):
    half = 0.5 * angle
    square = half * half
    series = jnp.full_like(square, 1.0)
    for n in (12, 10, 8, 6, 4, 2):
        series = 1.0 - series * square * (1.0 / (n * (n + 1)))
    sine = half * series
    return 1.0 - 2.0 * sine * sine


def mixed(w, own, other):
    rows = w.shape[0] // 2
    own_high, own_low = split(own)
    other_high, other_low = split(other)
    high = jnp.concatenate([own_high, other_high], axis=0)
    low = jnp.concatenate([own_low, other_low], axis=0)
    both = jnp.dot(w[...], high, preferred_element_type=jnp.float32)
    rest = jnp.dot(w[:rows], low, preferred_element_type=jnp.float32)
    return both[:rows] + (both[rows:] + rest)


def halves(first, second):
    lane = lax.broadcasted_iota(jnp.int32, first.shape, first.ndim - 1)
    near = lane < QUARTER
    turn = functools.partial(pltpu.roll, shift=QUARTER, axis=first.ndim - 1)
    return jnp.where(near, first, turn(second)), jnp.where(near, turn(first), second)


def scaled(value, angle):
    rank, width = angle.shape
    return (value.reshape(rank, SUB, width) * angle[:, None, :]).reshape(rank * SUB, width)


def kernel(
    units, rank, coeffs, phases_in, mixers_in, out, a, b, c_core, c_y, c_x, c_z, phases, mixers, weights, weights_two,
    cosines, z_cos, z_scale, small_sem, load_sem, core_send, core_recv, y_send, y_recv, x_send, x_recv, z_send, z_recv,
    back_send, back_recv, cos_send, cos_recv,
):
    wide, narrow = lax.axis_index("wide"), lax.axis_index("narrow")
    here, column = wide // 4, wide % 4
    core_peer, y_peer, x_peer = (wide, narrow ^ 1), (wide, narrow ^ 4), (wide ^ 2, narrow)
    half_lanes = coeffs.shape[2] // 2
    rows = rank * SUB

    def z_device(there):
        return there * 4 + column, narrow

    barrier = pltpu.get_barrier_semaphore()
    peers = [core_peer, y_peer, x_peer, *(z_device(here ^ p) for p in ORDER)]
    for peer in peers:
        pl.semaphore_signal(barrier, inc=1, device_id=peer, device_id_type=MESH)

    def window(ref, group, half, tile):
        columns = pl.ds(pl.multiple_of(group * SUB, SUB), SUB)
        return ref.at[:, columns, pl.ds(pl.multiple_of(half * half_lanes + tile * WIDTH, WIDTH), WIDTH)]

    def remote(src, dst, send, recv, peer):
        return pltpu.make_async_remote_copy(src, dst, send, recv, device_id=peer, device_id_type=MESH)

    def load(k, half):
        return pltpu.make_async_copy(window(coeffs, k // 4, half, k % 4), a.at[k, half], load_sem.at[k, half])

    def core_copy(k):
        return remote(a.at[k], c_core.at[k], core_send.at[k], core_recv.at[k], core_peer)

    def y_copy(k):
        return remote(b.at[k], c_y.at[k], y_send.at[k], y_recv.at[k], y_peer)

    def x_copy(k):
        return remote(a.at[k], c_x.at[k], x_send.at[k], x_recv.at[k], x_peer)

    def piece(ref, k, there):
        return ref.at[k, there // 2, pl.ds(there % 2 * (rank // 2), rank // 2)]

    def z_copy(k, p):
        there = here ^ p
        src, dst = piece(b, k, there), piece(c_z, k, here)
        return remote(src, dst, z_send.at[k, p - 1], z_recv.at[k, p - 1], z_device(there))

    def back_copy(k, p):
        there = here ^ p
        src, dst = piece(a, k, there), piece(c_core, k, here)
        return remote(src, dst, back_send.at[k, p - 1], back_recv.at[k, p - 1], z_device(there))

    def cos_copy(p):
        there = here ^ p
        src = cosines.at[:, :, there // 2, pl.ds(4, 2)]
        return remote(src, z_cos.at[here], cos_send.at[p - 1], cos_recv.at[p - 1], z_device(there))

    load_phases = pltpu.make_async_copy(phases_in, phases, small_sem.at[0])
    load_mixers = pltpu.make_async_copy(mixers_in, mixers, small_sem.at[1])
    load_mixers.start()
    load_phases.start()

    def fetch_own(k):
        for half in range(2):
            load(k, half).start()

    def share(k):
        for half in range(2):
            load(k, half).wait()
        core_copy(k).start()

    for k in range(FETCH):
        fetch_own(k)
    pl.semaphore_wait(barrier, len(peers))
    for k in range(SHARE):
        share(k)

    def take_cosines(level):
        value = cosine(phases[level])
        for tile in range(4):
            for half in range(2):
                start = half * half_lanes + tile * WIDTH
                cosines[tile // 2, tile % 2, half, level] = value[:, start : start + WIDTH]

    spread = (
        lax.broadcasted_iota(jnp.int32, (2 * rank, 2 * rows), 0)
        == lax.broadcasted_iota(jnp.int32, (2 * rank, 2 * rows), 1) // SUB
    ).astype(jnp.bfloat16)
    same_column = (
        lax.broadcasted_iota(jnp.int32, (2 * rows, 2 * rows), 0) % SUB
        == lax.broadcasted_iota(jnp.int32, (2 * rows, 2 * rows), 1) % SUB
    )

    def take_weights(slot, level, side):
        mixer = jnp.concatenate([mixers[level, side, side], mixers[level, side, 1 - side]], axis=1)
        parts = [
            jnp.broadcast_to(part.astype(jnp.float32)[:, None, :], (rank, SUB, 2 * rank)).reshape(rows, 2 * rank)
            for part in split(mixer)
        ]
        tall = jnp.concatenate(parts, axis=0).astype(jnp.bfloat16)
        wide_values = jnp.dot(tall, spread, preferred_element_type=jnp.float32)
        weights[slot] = jnp.where(same_column, wide_values, 0.0).astype(jnp.bfloat16)

    def take_weights_two(slot, level):
        mixer = jnp.concatenate(
            [jnp.concatenate([mixers[level, side, 0], mixers[level, side, 1]], axis=1) for side in range(2)], axis=0
        )
        for at, part in enumerate(split(mixer)):
            tall = jnp.broadcast_to(part.astype(jnp.float32)[:, None, :], (2 * rank, SUB, 2 * rank))
            tall = tall.reshape(2 * rows, 2 * rank).astype(jnp.bfloat16)
            wide_values = jnp.dot(tall, spread, preferred_element_type=jnp.float32)
            values = jnp.where(same_column, wide_values, 0.0).astype(jnp.bfloat16)
            weights_two[slot, at * 2 * rows : (at + 1) * 2 * rows] = values

    load_mixers.wait()
    take_weights(0, 0, narrow % 2)
    load_phases.wait()
    take_cosines(0)

    def both(ref, k):
        return jnp.concatenate([ref[k, 0].reshape(rows, WIDTH), ref[k, 1].reshape(rows, WIDTH)], axis=1)

    def put(ref, k, value):
        ref[k, 0] = value[:, :WIDTH].reshape(rank, SUB, WIDTH)
        ref[k, 1] = value[:, WIDTH:].reshape(rank, SUB, WIDTH)

    def angle(k, level, half):
        return cosines[k % 4 // 2, k % 2, half, level]

    def angles(k, level):
        return jnp.concatenate([angle(k, level, 0), angle(k, level, 1)], axis=1)

    def level_0(k):
        pl.when(k + FETCH < units)(lambda: fetch_own(k + FETCH))
        pl.when(k + SHARE < units)(lambda: share(k + SHARE))
        core_copy(k).wait()
        put(b, k, scaled(mixed(weights.at[0], both(a, k), both(c_core, k)), angles(k, 0)))
        y_copy(k).start()

    def levels_1_2(k):
        y_copy(k).wait_recv()
        value = scaled(mixed(weights.at[1], both(b, k), both(c_y, k)), angles(k, 1))
        value = mixed(weights_two.at[0], value[:, :WIDTH], value[:, WIDTH:])
        for half in range(2):
            part = scaled(value[half * rows : (half + 1) * rows], angle(k, 2, half))
            a[k, half] = part.reshape(rank, SUB, WIDTH)
        x_copy(k).start()

    def put_pieces(ref, k, half, tile):
        first, second = halves(tile[: rank // 2], tile[rank // 2 :])
        ref[k, half, : rank // 2] = first
        ref[k, half, rank // 2 :] = second

    def join(first, second):
        return jnp.concatenate(halves(first, second), axis=0)

    def level_3(k):
        x_copy(k).wait_recv()
        y_copy(k).wait_send()
        value = scaled(mixed(weights.at[2], both(a, k), both(c_x, k)), angles(k, 3))
        for half in range(2):
            put_pieces(b, k, half, value[:, half * WIDTH : (half + 1) * WIDTH].reshape(rank, SUB, WIDTH))
        for p in ORDER:
            z_copy(k, p).start()
        piece(c_z, k, here)[...] = piece(b, k, here)[...]

    def levels_4_5(k):
        for p in (1, 2, 3):
            z_copy(k, p).wait_recv()
        x_copy(k).wait_send()

        def z_piece(there):
            return c_z[k, there // 2, there % 2 * (rank // 2) : (there % 2 + 1) * (rank // 2)]

        def scale(n):
            return z_scale[k % 4 // 2, k % 2, n]

        even, odd = join(z_piece(0), z_piece(2)), join(z_piece(1), z_piece(3))
        value = mixed(weights_two.at[1], even.reshape(rows, WIDTH), odd.reshape(rows, WIDTH))
        low, high = halves(scaled(value[:rows], scale(0)), scaled(value[rows:], scale(1)))
        value = mixed(weights_two.at[2], low, high)
        for half in range(2):
            tile = scaled(value[half * rows : (half + 1) * rows], scale(2 + half))
            put_pieces(a, k, half, tile.reshape(rank, SUB, WIDTH))
        for p in ORDER:
            back_copy(k, p).start()
        piece(c_core, k, here)[...] = piece(a, k, here)[...]

    def result(k):
        for p in (1, 2, 3):
            back_copy(k, p).wait()
            z_copy(k, p).wait_send()
        for half in range(2):
            tile = join(c_core[k, half, : rank // 2], c_core[k, half, rank // 2 :])
            window(out, k // 4, half, k % 4)[...] = tile

    def take_z_scale():
        side = here % 2
        for tile in range(4):
            for level, pairs in enumerate((((0, 2), (1, 3)), ((0, 1), (2, 3)))):
                for at, pair in enumerate(pairs):
                    first, second = (z_cos[there, tile // 2, tile % 2, level] for there in pair)
                    near, far = halves(first, second)
                    z_scale[tile // 2, tile % 2, 2 * level + at] = jnp.where(side == 0, near, far)

    level_0(0)
    take_weights(1, 1, narrow // 4)
    take_cosines(1)
    level_0(1)
    take_cosines(2)
    take_weights_two(0, 2)
    level_0(2)

    def before_level_3():
        take_cosines(3)
        take_weights(2, 3, wide // 2 % 2)
        for level in (4, 5):
            take_cosines(level)
        for p in ORDER:
            cos_copy(p).start()
        z_cos[here] = cosines[:, :, here // 2, 4:6]

    def before_level_5():
        take_weights_two(1, 4)
        take_weights_two(2, 5)
        for p in (1, 2, 3):
            cos_copy(p).wait()
        take_z_scale()

    def finish(t):
        pl.when(t >= LAG_Z)(lambda: levels_4_5(t - LAG_Z))
        pl.when(t >= LAG_OUT)(lambda: result(t - LAG_OUT))

    def tick(t, carry):
        levels_1_2(t)
        finish(t)
        pl.when(t + AHEAD < units)(lambda: level_0(t + AHEAD))
        pl.when(t >= LAG_X)(lambda: level_3(t - LAG_X))
        pl.when(t == 0)(before_level_3)
        pl.when(t == LAG_Z - 1)(before_level_5)
        return carry

    def last(t, carry):
        finish(t)
        pl.when(t < units + LAG_X)(lambda: level_3(t - LAG_X))
        return carry

    def very_last(k, carry):
        result(k)
        return carry

    lax.fori_loop(0, units, tick, 0)
    lax.fori_loop(units, units + LAG_Z, last, 0)
    lax.fori_loop(units + LAG_Z - LAG_OUT, units, very_last, 0)


def write_out(parts, held, out, sems):
    depth = held.shape[0] // parts
    copies = [
        pltpu.make_async_copy(held.at[pl.ds(n * depth, depth)], out.at[pl.ds(n * depth, depth)], sems.at[n])
        for n in range(parts)
    ]
    for copy in copies:
        copy.start()
    for copy in copies:
        copy.wait()


def on_device(coeffs, phases, mixers):
    rank, columns, blocks = coeffs.shape
    levels = phases.shape[0]
    units = columns // SUB * (blocks // (2 * WIDTH))

    piece = pltpu.VMEM((units, 2, rank, SUB, WIDTH), jnp.float32)
    dma = pltpu.SemaphoreType.DMA
    any_space = pl.BlockSpec(memory_space=pl.ANY)
    vmem = pl.BlockSpec(memory_space=pltpu.VMEM)
    held = pl.pallas_call(
        functools.partial(kernel, units, rank),
        out_shape=pltpu.VMEM(coeffs.shape, coeffs.dtype),
        in_specs=[any_space, any_space, any_space],
        out_specs=vmem,
        scratch_shapes=[
            piece, piece, piece, piece, piece, piece,
            pltpu.VMEM(phases.shape, jnp.float32),
            pltpu.VMEM(mixers.shape, jnp.float32),
            pltpu.VMEM((3, 2 * rank * SUB, 2 * rank * SUB), jnp.bfloat16),
            pltpu.VMEM((3, 4 * rank * SUB, 2 * rank * SUB), jnp.bfloat16),
            pltpu.VMEM((2, 2, 2, levels, rank, WIDTH), jnp.float32),
            pltpu.VMEM((4, 2, 2, 2, rank, WIDTH), jnp.float32),
            pltpu.VMEM((2, 2, 4, rank, WIDTH), jnp.float32),
            dma((2,)), dma((units, 2)), dma((units,)), dma((units,)),
            dma((units,)), dma((units,)), dma((units,)), dma((units,)),
            dma((units, 3)), dma((units, 3)), dma((units, 3)), dma((units, 3)),
            dma((3,)), dma((3,)),
        ],
        compiler_params=pltpu.CompilerParams(
            collective_id=0, has_side_effects=True, vmem_limit_bytes=48 * 2**20
        ),
    )(coeffs, phases, mixers)
    return pl.pallas_call(
        functools.partial(write_out, 8),
        out_shape=jax.ShapeDtypeStruct(coeffs.shape, coeffs.dtype),
        in_specs=[any_space],
        out_specs=any_space,
        scratch_shapes=[dma((8,))],
        compiler_params=pltpu.CompilerParams(vmem_limit_bytes=2**20),
    )(held)


def solution(mesh):
    placed = (P(None, None, ("wide", "narrow")), P(None, None, ("wide", "narrow")), P())
    return jax.shard_map(
        on_device,
        mesh=mesh,
        in_specs=placed,
        out_specs=P(None, None, ("wide", "narrow")),
        check_vma=False,
    )
```
